32 devices in a mesh: groups: 2 (over x), corpus: 16 (over z, y, core).
Axes of the slice: x: 2, y: 2, z: 4, core: 2. Of those that a mesh axis runs over, the one named last changes fastest.
Arguments:
- queries: float32 [1024, 8192], P(('groups', 'corpus')), parts along dimension 0, may hold values from -6 to 6
- hinv_slots: float32 [32, 4096, 512], P(('groups', 'corpus')), parts along dimension 0, may hold values from -0.09375 to 0.09375
- block_of: int32 [32], P('groups'), parts along dimension 0, may hold values from 0 to 15, each once
- corpus_enc: bfloat16 [16384, 8192], P(('groups', 'corpus')), parts along dimension 0, may hold values from -0.0625 to 0.0625
Outputs:
- scores: float32 [512, 16384], P(None, ('groups', 'corpus')), parts along dimension 1
The draws below stay inside these ranges and needn't reach their ends.
There are 2 independent parts, one for each index of `groups`. The reference program is written for one: setup_inputs(seed, part) draws one part's arguments, and reference() takes and returns one part's arrays. A program takes and returns all parts, laid end to end along the dimension named above; each array names one. Nothing has to cross between parts.
Inputs may be any that keep to these rules, and one draw needn't show every extreme that they name: block_of names every column block exactly once.
All inputs are finite; a program needn't handle non-finite values.
Results may differ from the reference program's by a relative error of at most 0.003.
Values may be sent and summed in bfloat16 or wider, within the bound.
A program may use at most 128 MiB of HBM per device.

```python
import jax
import jax.numpy as jnp
from jax import lax

MODULES = 2
MW = 4096
E = 8192
NQ = 512
NC = 8192
BW = 512
NB = 16


def levels(rng, shape, split, least, high):
    loudness = 1.0
    for axis_at, parts in split:
        draws = jax.random.uniform(jax.random.fold_in(jax.random.fold_in(rng, 6), axis_at), (parts,), jnp.float32, least / len(split), high / len(split))
        loudness = loudness * jnp.repeat(jnp.exp(draws), shape[axis_at] // parts).reshape((-1,) + (1,) * (len(shape) - 1 - axis_at))
    return loudness


def centred(rng, extent, scale, bound, cuts=(), kind=jnp.bfloat16):
    level = levels(rng, extent, cuts, -0.22, 0.18) if cuts else 1.0
    drawn = jax.random.normal(rng, extent, jnp.float32) * scale * level
    return jnp.minimum(jnp.maximum(drawn, -bound), bound).astype(kind)


def setup_inputs(seed: int = 0, part: int = 0) -> dict:
    splits = jax.random.split(jax.random.key(seed), 5)
    part_splits = jax.random.split(jax.random.fold_in(splits[4], part), 5)
    queries = centred(part_splits[0], (NQ, E), 1.0, 6.0, ((0, 16),), jnp.float32)
    hinv_slots = centred(part_splits[1], (NB, MW, BW), MW ** -0.5, 0.09375, ((0, 16),), jnp.float32)
    block_of = jax.random.permutation(part_splits[2], NB).astype(jnp.int32)
    corpus_enc = centred(part_splits[3], (NC, E), E ** -0.5, 0.0625, ((0, 16),))
    return {"queries": queries, "hinv_slots": hinv_slots, "block_of": block_of, "corpus_enc": corpus_enc}


def reference(queries, hinv_slots, block_of, corpus_enc):
    slots, mod_width, block_width = hinv_slots.shape
    per_module = mod_width // block_width
    ordered = jnp.zeros_like(hinv_slots).at[block_of].set(hinv_slots)
    inverse = ordered.reshape(MODULES, per_module, mod_width, block_width)
    inverse = inverse.transpose(0, 2, 1, 3).reshape(MODULES, mod_width, mod_width)
    rows = queries.shape[0]
    folded = jnp.einsum("qmi,mij->qmj", queries.reshape(rows, MODULES, mod_width), inverse, precision=lax.Precision.HIGHEST)
    precond = folded.reshape(rows, MODULES * mod_width).astype(jnp.bfloat16)
    return jnp.dot(precond, corpus_enc.T, preferred_element_type=jnp.float32)
```

```python
import jax
import jax.numpy as jnp
from jax import lax
from jax.experimental import pallas as pl
from jax.experimental.pallas import tpu as pltpu
from jax.sharding import PartitionSpec as P

RING = 8
PARTS = 4
MESH = pl.DeviceIdType.MESH


def by_collectives(queries, hinv_slots, block_of, corpus_enc):
    width = queries.shape[1]
    mod_width = hinv_slots.shape[1]
    block_width = hinv_slots.shape[2]
    per_module = mod_width // block_width
    slots = block_of.shape[0]
    me = lax.axis_index("corpus")
    gathered = lax.all_gather(queries.astype(jnp.bfloat16), "corpus", axis=0, tiled=True)
    order = jnp.arange(slots, dtype=block_of.dtype)
    my_block = jnp.sum(jnp.where(order == me, block_of, 0))
    mine = jnp.where(
        my_block // per_module == 0, gathered[:, :mod_width], gathered[:, mod_width:]
    )
    block = hinv_slots[0]
    high = block.astype(jnp.bfloat16)
    low = (block - high.astype(jnp.float32)).astype(jnp.bfloat16)
    part = jnp.dot(mine, high, preferred_element_type=jnp.float32)
    part += jnp.dot(mine, low, preferred_element_type=jnp.float32)
    parts = lax.all_gather(part.astype(jnp.bfloat16), "corpus", axis=0)
    placing = (block_of[:, None] == order[None, :]).astype(jnp.bfloat16)
    precond = jnp.einsum(
        "srj,sb->rbj", parts, placing, preferred_element_type=jnp.float32
    ).astype(jnp.bfloat16).reshape(-1, width)
    return lax.dot_general(
        precond, corpus_enc, (((1,), (1,)), ((), ())), preferred_element_type=jnp.float32
    )


def kernel(
    block_of, q_hbm, h_hbm, c_hbm, out,
    q_wide, h_wide, h_high, h_low, corpus, qbuf, pbuf, acc,
    load_sem, corpus_sem, q_ring_send, q_ring_recv, q_pair_send, q_pair_recv,
    p_ring_send, p_ring_recv, p_pair_send, p_pair_recv,
):
    rows = q_hbm.shape[0]
    mod_width, block_width = h_hbm.shape[1], h_hbm.shape[2]
    per_module = mod_width // block_width
    half = rows // 2
    depth = mod_width // PARTS
    part_rows = pbuf.shape[1] // PARTS

    me = lax.axis_index("corpus")
    core = me % 2
    across = (me // 2) % 2
    along = me // 4
    pos = along + across * (RING - 1 - 2 * along)

    def device(position, which):
        position = (position + 2 * RING) % RING
        y = position // (RING // 2)
        z = position + y * (RING - 1 - 2 * position)
        return z * 4 + y * 2 + which

    ahead = device(pos + 1 - 2 * core, core)
    behind = device(pos - 1 + 2 * core, core)
    pair = me + 1 - 2 * core

    load_q = pltpu.make_async_copy(q_hbm, q_wide, load_sem.at[0])
    load_q.start()
    load_h = [
        pltpu.make_async_copy(
            h_hbm.at[0, pl.ds(k * depth, depth)], h_wide.at[pl.ds(k * depth, depth)], load_sem.at[1 + k]
        )
        for k in range(PARTS)
    ]
    for copy in load_h:
        copy.start()
    slots = corpus.shape[0]
    load_c = [
        pltpu.make_async_copy(
            c_hbm.at[:, pl.ds(b * block_width, block_width)], corpus.at[b], corpus_sem.at[b]
        )
        for b in range(slots)
    ]
    for copy in load_c:
        copy.start()

    barrier = pltpu.get_barrier_semaphore()
    for other in (ahead, behind, pair):
        pl.semaphore_signal(barrier, inc=1, device_id={"corpus": other}, device_id_type=MESH)

    load_q.wait()
    for j in range(2):
        qbuf[j, core] = q_wide[:, j * mod_width:(j + 1) * mod_width].astype(jnp.bfloat16)
    out[...] = jnp.zeros_like(out)
    pl.semaphore_wait(barrier, 3)

    def q_piece(slot, k):
        return qbuf.at[k // 2, slot, pl.ds((k % 2) * half, half)]

    def q_ring(s, k):
        return pltpu.make_async_remote_copy(
            src_ref=q_piece(2 * s + core, k), dst_ref=q_piece(2 * s + 2 + core, k),
            send_sem=q_ring_send.at[s, k], recv_sem=q_ring_recv.at[s, k],
            device_id={"corpus": ahead}, device_id_type=MESH,
        )

    def q_pair(s, k, which):
        return pltpu.make_async_remote_copy(
            src_ref=q_piece(2 * s + which, k), dst_ref=q_piece(2 * s + which, k),
            send_sem=q_pair_send.at[s, k], recv_sem=q_pair_recv.at[s, k],
            device_id={"corpus": pair}, device_id_type=MESH,
        )

    def p_piece(slot, k):
        return pbuf.at[slot, pl.ds(k * part_rows, part_rows)]

    def p_ring(s, k):
        return pltpu.make_async_remote_copy(
            src_ref=p_piece(2 * s + core, k), dst_ref=p_piece(2 * s + 2 + core, k),
            send_sem=p_ring_send.at[s, k], recv_sem=p_ring_recv.at[s, k],
            device_id={"corpus": ahead}, device_id_type=MESH,
        )

    def p_pair(s, k, which):
        return pltpu.make_async_remote_copy(
            src_ref=p_piece(2 * s + which, k), dst_ref=p_piece(2 * s + which, k),
            send_sem=p_pair_send.at[s, k], recv_sem=p_pair_recv.at[s, k],
            device_id={"corpus": pair}, device_id_type=MESH,
        )

    for k in range(PARTS):
        q_ring(0, k).start()
    for k in range(PARTS):
        q_pair(0, k, core).start()

    for k in range(PARTS):
        load_h[k].wait()

        def split(i, carry, k=k):
            at = pl.ds(pl.multiple_of(k * depth + i * 128, 128), 128)
            wide = h_wide[at]
            high = wide.astype(jnp.bfloat16)
            h_high[at] = high
            h_low[at] = (wide - high.astype(jnp.float32)).astype(jnp.bfloat16)
            return carry

        lax.fori_loop(0, depth // 128, split, 0)

    second = (block_of[me] // per_module).astype(jnp.float32)
    weight = ((1.0 - second).astype(jnp.bfloat16), second.astype(jnp.bfloat16))

    def fold(s, k):
        pick = (
            qbuf[0, pl.ds(2 * s, 2), :, k * depth:(k + 1) * depth] * weight[0]
            + qbuf[1, pl.ds(2 * s, 2), :, k * depth:(k + 1) * depth] * weight[1]
        ).reshape(2 * rows, depth)
        at = slice(k * depth, (k + 1) * depth)
        total = jnp.dot(pick, h_high[at], preferred_element_type=jnp.float32)
        total += jnp.dot(pick, h_low[at], preferred_element_type=jnp.float32)
        if k == 0:
            acc[...] = total
        elif k < PARTS - 1:
            acc[...] += total
        else:
            at = pl.ds(pl.multiple_of(s * 2 * rows, 2 * rows), 2 * rows)
            pbuf[core, at] = (acc[...] + total).astype(jnp.bfloat16)

    def pair_arrived(s):
        for k in range(PARTS):
            q_pair(s, k, 1 - core).wait_recv()

    def q_step(s, carry):
        pair_arrived(s - 1)
        for k in range(PARTS):
            q_ring(s - 1, k).wait_recv()
            q_ring(s, k).start()
            q_pair(s, k, core).start()
            fold(s - 1, k)
        return carry

    lax.fori_loop(1, RING - 1, q_step, 0)

    for k in range(PARTS - 1):
        p_ring(0, k).start()
        p_pair(0, k, core).start()
    last = RING - 1
    pair_arrived(last - 1)
    for k in range(PARTS):
        q_ring(last - 1, k).wait_recv()
        q_pair(last, k, core).start()
        fold(last - 1, k)
    pair_arrived(last)
    for k in range(PARTS):
        fold(last, k)
    p_ring(0, PARTS - 1).start()
    p_pair(0, PARTS - 1, core).start()
    for copy in load_c:
        copy.wait()

    def score(s, which):
        origin = pos - s + 2 * s * which
        block = block_of[device(origin, which)]
        result = lax.dot_general(
            pbuf[2 * s + which], corpus[block], (((1,), (1,)), ((), ())),
            preferred_element_type=jnp.float32,
        )
        for t in range(RING):
            for w in range(2):
                row = device(origin - t + 2 * t * w, w) * rows
                cut = (2 * t + w) * rows
                out[pl.ds(pl.multiple_of(row, rows), rows)] += result[cut:cut + rows]

    def p_arrived(s):
        for k in range(PARTS):
            p_pair(s, k, 1 - core).wait_recv()

    def p_step(s, carry):
        for k in range(PARTS):
            p_ring(s - 1, k).wait_recv()
            p_ring(s, k).start()
            p_pair(s, k, core).start()
            if k == 1:
                score(s - 1, core)
        p_arrived(s - 1)
        score(s - 1, 1 - core)
        return carry

    lax.fori_loop(1, RING - 1, p_step, 0)
    for k in range(PARTS):
        p_ring(last - 1, k).wait_recv()
        p_pair(last, k, core).start()
        if k == 1:
            score(last - 1, core)
    p_arrived(last - 1)
    score(last - 1, 1 - core)
    score(last, core)
    p_arrived(last)
    score(last, 1 - core)

    def sent(s, carry):
        for k in range(PARTS):
            q_pair(s, k, core).wait_send()
            p_pair(s, k, core).wait_send()
        return carry

    def ring_sent(s, carry):
        for k in range(PARTS):
            q_ring(s, k).wait_send()
            p_ring(s, k).wait_send()
        return carry

    lax.fori_loop(0, RING, sent, 0)
    lax.fori_loop(0, RING - 1, ring_sent, 0)


def by_kernel(queries, hinv_slots, block_of, corpus_enc):
    rows, width = queries.shape
    _, mod_width, block_width = hinv_slots.shape
    held = corpus_enc.shape[0]
    slots = 2 * RING
    total = slots * rows
    sems = pltpu.SemaphoreType.DMA((RING, PARTS))
    anywhere = pl.BlockSpec(memory_space=pl.ANY)
    return pl.pallas_call(
        kernel,
        out_shape=jax.ShapeDtypeStruct((total, held), jnp.float32),
        in_specs=[pl.BlockSpec(memory_space=pltpu.SMEM), anywhere, anywhere, anywhere],
        out_specs=pl.BlockSpec(memory_space=pltpu.VMEM),
        scratch_shapes=[
            pltpu.VMEM((rows, width), jnp.float32),
            pltpu.VMEM((mod_width, block_width), jnp.float32),
            pltpu.VMEM((mod_width, block_width), jnp.bfloat16),
            pltpu.VMEM((mod_width, block_width), jnp.bfloat16),
            pltpu.VMEM((slots, held, block_width), jnp.bfloat16),
            pltpu.VMEM((2, slots, rows, mod_width), jnp.bfloat16),
            pltpu.VMEM((slots, total, block_width), jnp.bfloat16),
            pltpu.VMEM((2 * rows, block_width), jnp.float32),
            pltpu.SemaphoreType.DMA((1 + PARTS,)),
            pltpu.SemaphoreType.DMA((slots,)),
        ] + [sems] * 8,
        compiler_params=pltpu.CompilerParams(
            collective_id=0, has_side_effects=True, vmem_limit_bytes=58 * 2**20
        ),
        cost_estimate=pl.CostEstimate(
            flops=2 * total * block_width * mod_width * 2 + 2 * total * held * width,
            bytes_accessed=20 * 2**20, transcendentals=0,
        ),
    )(block_of, queries, hinv_slots, corpus_enc)


def solution(mesh):
    devices = mesh.shape["corpus"]

    def on_device(queries, hinv_slots, block_of, corpus_enc):
        fits = (
            devices == 2 * RING
            and queries.shape[0] % 32 == 0
            and queries.shape[1] == 2 * hinv_slots.shape[1]
            and hinv_slots.shape[2] % 128 == 0
        )
        body = by_kernel if fits else by_collectives
        return body(queries, hinv_slots, block_of, corpus_enc)

    return jax.shard_map(
        on_device,
        mesh=mesh,
        in_specs=(
            P(("groups", "corpus"), None),
            P(("groups", "corpus"), None, None),
            P("groups"),
            P(("groups", "corpus"), None),
        ),
        out_specs=P(None, ("groups", "corpus")),
        check_vma=False,
    )
```

```python
import jax
import jax.numpy as jnp
from jax import lax
from jax.experimental import pallas as pl
from jax.experimental.pallas import tpu as pltpu
from jax.sharding import PartitionSpec as P

RING = 8
PARTS = 4
MESH = pl.DeviceIdType.MESH


def by_collectives(queries, hinv_slots, block_of, corpus_enc):
    width = queries.shape[1]
    mod_width = hinv_slots.shape[1]
    block_width = hinv_slots.shape[2]
    per_module = mod_width // block_width
    slots = block_of.shape[0]
    me = lax.axis_index("corpus")
    gathered = lax.all_gather(queries.astype(jnp.bfloat16), "corpus", axis=0, tiled=True)
    order = jnp.arange(slots, dtype=block_of.dtype)
    my_block = jnp.sum(jnp.where(order == me, block_of, 0))
    mine = jnp.where(
        my_block // per_module == 0, gathered[:, :mod_width], gathered[:, mod_width:]
    )
    block = hinv_slots[0]
    high = block.astype(jnp.bfloat16)
    low = (block - high.astype(jnp.float32)).astype(jnp.bfloat16)
    part = jnp.dot(mine, high, preferred_element_type=jnp.float32)
    part += jnp.dot(mine, low, preferred_element_type=jnp.float32)
    parts = lax.all_gather(part.astype(jnp.bfloat16), "corpus", axis=0)
    placing = (block_of[:, None] == order[None, :]).astype(jnp.bfloat16)
    precond = jnp.einsum(
        "srj,sb->rbj", parts, placing, preferred_element_type=jnp.float32
    ).astype(jnp.bfloat16).reshape(-1, width)
    return lax.dot_general(
        precond, corpus_enc, (((1,), (1,)), ((), ())), preferred_element_type=jnp.float32
    )


def kernel(
    block_of, q_hbm, h_hbm, c_hbm, out,
    q_wide, h_wide, h_high, h_low, corpus, qbuf, pbuf, acc,
    load_sem, corpus_sem, q_ring_send, q_ring_recv, q_pair_send, q_pair_recv,
    p_ring_send, p_ring_recv, p_pair_send, p_pair_recv,
):
    rows = q_hbm.shape[0]
    mod_width, block_width = h_hbm.shape[1], h_hbm.shape[2]
    per_module = mod_width // block_width
    half = rows // 2
    depth = mod_width // PARTS
    part_rows = pbuf.shape[1] // PARTS

    me = lax.axis_index("corpus")
    core = me % 2
    across = (me // 2) % 2
    along = me // 4
    pos = along + across * (RING - 1 - 2 * along)

    def device(position, which):
        position = (position + 2 * RING) % RING
        y = position // (RING // 2)
        z = position + y * (RING - 1 - 2 * position)
        return z * 4 + y * 2 + which

    ahead = device(pos + 1 - 2 * core, core)
    behind = device(pos - 1 + 2 * core, core)
    pair = me + 1 - 2 * core

    load_q = [
        pltpu.make_async_copy(
            q_hbm.at[pl.ds((k % 2) * half, half), pl.ds((k // 2) * mod_width, mod_width)],
            q_wide.at[pl.ds((k % 2) * half, half), pl.ds((k // 2) * mod_width, mod_width)],
            load_sem.at[k],
        )
        for k in range(PARTS)
    ]
    for copy in load_q:
        copy.start()
    barrier = pltpu.get_barrier_semaphore()
    for other in (ahead, behind, pair):
        pl.semaphore_signal(barrier, inc=1, device_id={"corpus": other}, device_id_type=MESH)
    load_h = [
        pltpu.make_async_copy(
            h_hbm.at[0, pl.ds(k * depth, depth)], h_wide.at[pl.ds(k * depth, depth)], load_sem.at[PARTS + k]
        )
        for k in range(PARTS)
    ]
    slots = corpus.shape[0]
    load_c = [
        pltpu.make_async_copy(
            c_hbm.at[:, pl.ds(b * block_width, block_width)], corpus.at[b], corpus_sem.at[b]
        )
        for b in range(slots)
    ]

    def q_piece(slot, k):
        return qbuf.at[k // 2, slot, pl.ds((k % 2) * half, half)]

    def q_ring(s, k):
        return pltpu.make_async_remote_copy(
            src_ref=q_piece(2 * s + core, k), dst_ref=q_piece(2 * s + 2 + core, k),
            send_sem=q_ring_send.at[s, k], recv_sem=q_ring_recv.at[s, k],
            device_id={"corpus": ahead}, device_id_type=MESH,
        )

    def q_pair(s, k, which):
        return pltpu.make_async_remote_copy(
            src_ref=q_piece(2 * s + which, k), dst_ref=q_piece(2 * s + which, k),
            send_sem=q_pair_send.at[s, k], recv_sem=q_pair_recv.at[s, k],
            device_id={"corpus": pair}, device_id_type=MESH,
        )

    def p_piece(slot, k):
        return pbuf.at[slot, pl.ds(k * part_rows, part_rows)]

    def p_ring(s, k):
        return pltpu.make_async_remote_copy(
            src_ref=p_piece(2 * s + core, k), dst_ref=p_piece(2 * s + 2 + core, k),
            send_sem=p_ring_send.at[s, k], recv_sem=p_ring_recv.at[s, k],
            device_id={"corpus": ahead}, device_id_type=MESH,
        )

    def p_pair(s, k, which):
        return pltpu.make_async_remote_copy(
            src_ref=p_piece(2 * s + which, k), dst_ref=p_piece(2 * s + which, k),
            send_sem=p_pair_send.at[s, k], recv_sem=p_pair_recv.at[s, k],
            device_id={"corpus": pair}, device_id_type=MESH,
        )

    for k in range(PARTS):
        load_q[k].wait()
        held_rows = slice((k % 2) * half, (k % 2 + 1) * half)
        held_columns = slice((k // 2) * mod_width, (k // 2 + 1) * mod_width)
        qbuf[k // 2, core, held_rows] = q_wide[held_rows, held_columns].astype(jnp.bfloat16)
        if k == 0:
            pl.semaphore_wait(barrier, 3)
        q_ring(0, k).start()
        q_pair(0, k, core).start()
    for copy in load_h + load_c:
        copy.start()
    out[...] = jnp.zeros_like(out)

    def split_part(k):
        def split(i, carry):
            at = pl.ds(pl.multiple_of(k * depth + i * 128, 128), 128)
            wide = h_wide[at]
            high = wide.astype(jnp.bfloat16)
            h_high[at] = high
            h_low[at] = (wide - high.astype(jnp.float32)).astype(jnp.bfloat16)
            return carry

        lax.fori_loop(0, depth // 128, split, 0)

    second = (block_of[me] // per_module).astype(jnp.float32)
    weight = ((1.0 - second).astype(jnp.bfloat16), second.astype(jnp.bfloat16))

    def fold(s, k):
        pick = (
            qbuf[0, pl.ds(2 * s, 2), :, k * depth:(k + 1) * depth] * weight[0]
            + qbuf[1, pl.ds(2 * s, 2), :, k * depth:(k + 1) * depth] * weight[1]
        ).reshape(2 * rows, depth)
        at = slice(k * depth, (k + 1) * depth)
        total = jnp.dot(pick, h_high[at], preferred_element_type=jnp.float32)
        total += jnp.dot(pick, h_low[at], preferred_element_type=jnp.float32)
        if k == 0:
            acc[...] = total
        elif k < PARTS - 1:
            acc[...] += total
        else:
            at = pl.ds(pl.multiple_of(s * 2 * rows, 2 * rows), 2 * rows)
            pbuf[core, at] = (acc[...] + total).astype(jnp.bfloat16)

    def pair_arrived(s):
        for k in range(PARTS):
            q_pair(s, k, 1 - core).wait_recv()

    def q_step(s, carry):
        pair_arrived(s - 1)
        for k in range(PARTS):
            q_ring(s - 1, k).wait_recv()
            q_ring(s, k).start()
            q_pair(s, k, core).start()
            fold(s - 1, k)
        return carry

    for k in range(PARTS):
        q_ring(0, k).wait_recv()
        q_ring(1, k).start()
        q_pair(1, k, core).start()
        load_h[k].wait()
        split_part(k)
        if k == 0:
            pair_arrived(0)
        fold(0, k)
    lax.fori_loop(2, RING - 1, q_step, 0)

    for k in range(PARTS - 1):
        p_ring(0, k).start()
        p_pair(0, k, core).start()
    last = RING - 1
    pair_arrived(last - 1)
    for k in range(PARTS):
        q_ring(last - 1, k).wait_recv()
        q_pair(last, k, core).start()
        fold(last - 1, k)
    pair_arrived(last)
    for k in range(PARTS):
        fold(last, k)
    p_ring(0, PARTS - 1).start()
    p_pair(0, PARTS - 1, core).start()
    for copy in load_c:
        copy.wait()

    def score(s, which, low=0, high=PARTS):
        origin = pos - s + 2 * s * which
        block = block_of[device(origin, which)]
        start = low * part_rows
        result = lax.dot_general(
            pbuf[2 * s + which, start:high * part_rows], corpus[block], (((1,), (1,)), ((), ())),
            preferred_element_type=jnp.float32,
        )
        for i in range((high - low) * part_rows // rows):
            t, w = (start // rows + i) // 2, i % 2
            row = device(origin - t + 2 * t * w, w) * rows
            out[pl.ds(pl.multiple_of(row, rows), rows)] += result[i * rows:(i + 1) * rows]

    def p_arrived(s, low=0, high=PARTS):
        for k in range(low, high):
            p_pair(s, k, 1 - core).wait_recv()

    def p_step(s, carry):
        for k in range(PARTS):
            p_ring(s - 1, k).wait_recv()
            p_ring(s, k).start()
            p_pair(s, k, core).start()
            q_ring(s - 1, k).wait_send()
            q_pair(s - 1, k, core).wait_send()
            if k == 1:
                score(s - 1, core)
        p_arrived(s - 1)
        score(s - 1, 1 - core)
        return carry

    lax.fori_loop(1, last, p_step, 0)

    def p_sent(s, carry):
        for k in range(PARTS):
            p_ring(s, k).wait_send()
            p_pair(s, k, core).wait_send()
        return carry

    middle = PARTS // 2
    for k in range(PARTS):
        p_ring(last - 1, k).wait_recv()
        p_pair(last, k, core).start()
        if k == 0:
            score(last - 1, core)
            for i in range(PARTS):
                q_ring(last - 1, i).wait_send()
                q_pair(last - 1, i, core).wait_send()
                q_pair(last, i, core).wait_send()
        elif k == 1:
            p_arrived(last - 1)
            score(last - 1, 1 - core)
            lax.fori_loop(0, last - 2, p_sent, 0)
        elif k == 2:
            score(last, core, 0, middle)
            p_arrived(last, 0, middle)
            score(last, 1 - core, 0, middle)
    score(last, core, middle, PARTS)
    p_arrived(last, middle, PARTS)
    score(last, 1 - core, middle, PARTS)
    lax.fori_loop(last - 2, last, p_sent, 0)
    for k in range(PARTS):
        p_pair(last, k, core).wait_send()


def by_kernel(queries, hinv_slots, block_of, corpus_enc):
    rows, width = queries.shape
    _, mod_width, block_width = hinv_slots.shape
    held = corpus_enc.shape[0]
    slots = 2 * RING
    total = slots * rows
    sems = pltpu.SemaphoreType.DMA((RING, PARTS))
    anywhere = pl.BlockSpec(memory_space=pl.ANY)
    return pl.pallas_call(
        kernel,
        out_shape=pltpu.VMEM((total, held), jnp.float32),
        in_specs=[pl.BlockSpec(memory_space=pltpu.SMEM), anywhere, anywhere, anywhere],
        out_specs=pl.BlockSpec(memory_space=pltpu.VMEM),
        scratch_shapes=[
            pltpu.VMEM((rows, width), jnp.float32),
            pltpu.VMEM((mod_width, block_width), jnp.float32),
            pltpu.VMEM((mod_width, block_width), jnp.bfloat16),
            pltpu.VMEM((mod_width, block_width), jnp.bfloat16),
            pltpu.VMEM((slots, held, block_width), jnp.bfloat16),
            pltpu.VMEM((2, slots, rows, mod_width), jnp.bfloat16),
            pltpu.VMEM((slots, total, block_width), jnp.bfloat16),
            pltpu.VMEM((2 * rows, block_width), jnp.float32),
            pltpu.SemaphoreType.DMA((2 * PARTS,)),
            pltpu.SemaphoreType.DMA((slots,)),
        ] + [sems] * 8,
        compiler_params=pltpu.CompilerParams(
            collective_id=0, has_side_effects=True, vmem_limit_bytes=61 * 2**20
        ),
        cost_estimate=pl.CostEstimate(
            flops=2 * total * block_width * mod_width * 2 + 2 * total * held * width,
            bytes_accessed=20 * 2**20, transcendentals=0,
        ),
    )(block_of, queries, hinv_slots, corpus_enc)


def solution(mesh):
    devices = mesh.shape["corpus"]

    def on_device(queries, hinv_slots, block_of, corpus_enc):
        fits = (
            devices == 2 * RING
            and queries.shape[0] % 32 == 0
            and queries.shape[1] == 2 * hinv_slots.shape[1]
            and hinv_slots.shape[2] % 128 == 0
        )
        body = by_kernel if fits else by_collectives
        return body(queries, hinv_slots, block_of, corpus_enc)

    return jax.shard_map(
        on_device,
        mesh=mesh,
        in_specs=(
            P(("groups", "corpus"), None),
            P(("groups", "corpus"), None, None),
            P("groups"),
            P(("groups", "corpus"), None),
        ),
        out_specs=P(None, ("groups", "corpus")),
        check_vma=False,
    )
```

```python
import jax
import jax.numpy as jnp
from jax import lax
from jax.experimental import pallas as pl
from jax.experimental.pallas import tpu as pltpu
from jax.sharding import PartitionSpec as P

RING = 8
PARTS = 4
MESH = pl.DeviceIdType.MESH


def by_collectives(queries, hinv_slots, block_of, corpus_enc):
    width = queries.shape[1]
    mod_width = hinv_slots.shape[1]
    block_width = hinv_slots.shape[2]
    per_module = mod_width // block_width
    slots = block_of.shape[0]
    me = lax.axis_index("corpus")
    gathered = lax.all_gather(queries.astype(jnp.bfloat16), "corpus", axis=0, tiled=True)
    order = jnp.arange(slots, dtype=block_of.dtype)
    my_block = jnp.sum(jnp.where(order == me, block_of, 0))
    mine = jnp.where(
        my_block // per_module == 0, gathered[:, :mod_width], gathered[:, mod_width:]
    )
    block = hinv_slots[0]
    high = block.astype(jnp.bfloat16)
    low = (block - high.astype(jnp.float32)).astype(jnp.bfloat16)
    part = jnp.dot(mine, high, preferred_element_type=jnp.float32)
    part += jnp.dot(mine, low, preferred_element_type=jnp.float32)
    parts = lax.all_gather(part.astype(jnp.bfloat16), "corpus", axis=0)
    placing = (block_of[:, None] == order[None, :]).astype(jnp.bfloat16)
    precond = jnp.einsum(
        "srj,sb->rbj", parts, placing, preferred_element_type=jnp.float32
    ).astype(jnp.bfloat16).reshape(-1, width)
    return lax.dot_general(
        precond, corpus_enc, (((1,), (1,)), ((), ())), preferred_element_type=jnp.float32
    )


def kernel(
    block_of, q_hbm, h_hbm, c_hbm, out,
    q_wide, h_wide, h_high, h_low, corpus, qbuf, pbuf, acc,
    load_sem, corpus_sem, q_ring_send, q_ring_recv, q_pair_send, q_pair_recv,
    p_ring_send, p_ring_recv, p_pair_send, p_pair_recv,
):
    rows = q_hbm.shape[0]
    mod_width, block_width = h_hbm.shape[1], h_hbm.shape[2]
    per_module = mod_width // block_width
    half = rows // 2
    depth = mod_width // PARTS
    part_rows = pbuf.shape[1] // PARTS

    me = lax.axis_index("corpus")
    core = me % 2
    across = (me // 2) % 2
    along = me // 4
    pos = along + across * (RING - 1 - 2 * along)

    def device(position, which):
        position = (position + 2 * RING) % RING
        y = position // (RING // 2)
        z = position + y * (RING - 1 - 2 * position)
        return z * 4 + y * 2 + which

    ahead = device(pos + 1 - 2 * core, core)
    behind = device(pos - 1 + 2 * core, core)
    pair = me + 1 - 2 * core

    barrier = pltpu.get_barrier_semaphore()
    for other in (ahead, behind, pair):
        pl.semaphore_signal(barrier, inc=1, device_id={"corpus": other}, device_id_type=MESH)
    load_q = [
        pltpu.make_async_copy(
            q_hbm.at[pl.ds((k % 2) * half, half), pl.ds((k // 2) * mod_width, mod_width)],
            q_wide.at[pl.ds((k % 2) * half, half), pl.ds((k // 2) * mod_width, mod_width)],
            load_sem.at[k],
        )
        for k in range(PARTS)
    ]
    for copy in load_q:
        copy.start()
    load_h = [
        pltpu.make_async_copy(
            h_hbm.at[0, pl.ds(k * depth, depth)], h_wide.at[pl.ds(k * depth, depth)], load_sem.at[PARTS + k]
        )
        for k in range(PARTS)
    ]
    slots = corpus.shape[0]
    load_c = [
        pltpu.make_async_copy(
            c_hbm.at[:, pl.ds(b * block_width, block_width)], corpus.at[b], corpus_sem.at[b]
        )
        for b in range(slots)
    ]

    def q_piece(slot, k):
        return qbuf.at[k // 2, slot, pl.ds((k % 2) * half, half)]

    def q_ring(s, k):
        return pltpu.make_async_remote_copy(
            src_ref=q_piece(2 * s + core, k), dst_ref=q_piece(2 * s + 2 + core, k),
            send_sem=q_ring_send.at[s, k], recv_sem=q_ring_recv.at[s, k],
            device_id={"corpus": ahead}, device_id_type=MESH,
        )

    def q_pair(s, k, which):
        return pltpu.make_async_remote_copy(
            src_ref=q_piece(2 * s + which, k), dst_ref=q_piece(2 * s + which, k),
            send_sem=q_pair_send.at[s, k], recv_sem=q_pair_recv.at[s, k],
            device_id={"corpus": pair}, device_id_type=MESH,
        )

    def p_piece(slot, k):
        return pbuf.at[slot, pl.ds(k * part_rows, part_rows)]

    def p_ring(s, k):
        return pltpu.make_async_remote_copy(
            src_ref=p_piece(2 * s + core, k), dst_ref=p_piece(2 * s + 2 + core, k),
            send_sem=p_ring_send.at[s, k], recv_sem=p_ring_recv.at[s, k],
            device_id={"corpus": ahead}, device_id_type=MESH,
        )

    def p_pair(s, k, which):
        return pltpu.make_async_remote_copy(
            src_ref=p_piece(2 * s + which, k), dst_ref=p_piece(2 * s + which, k),
            send_sem=p_pair_send.at[s, k], recv_sem=p_pair_recv.at[s, k],
            device_id={"corpus": pair}, device_id_type=MESH,
        )

    for k in range(PARTS):
        load_q[k].wait()
        held_rows = slice((k % 2) * half, (k % 2 + 1) * half)
        held_columns = slice((k // 2) * mod_width, (k // 2 + 1) * mod_width)
        qbuf[k // 2, core, held_rows] = q_wide[held_rows, held_columns].astype(jnp.bfloat16)
        if k == 0:
            pl.semaphore_wait(barrier, 3)
        q_ring(0, k).start()
        q_pair(0, k, core).start()
    for copy in load_h + load_c:
        copy.start()
    out[...] = jnp.zeros_like(out)

    def split_part(k):
        def split(i, carry):
            at = pl.ds(pl.multiple_of(k * depth + i * 128, 128), 128)
            wide = h_wide[at]
            high = wide.astype(jnp.bfloat16)
            h_high[at] = high
            h_low[at] = (wide - high.astype(jnp.float32)).astype(jnp.bfloat16)
            return carry

        lax.fori_loop(0, depth // 128, split, 0)

    second = (block_of[me] // per_module).astype(jnp.float32)
    weight = ((1.0 - second).astype(jnp.bfloat16), second.astype(jnp.bfloat16))

    def fold(s, k):
        pick = (
            qbuf[0, pl.ds(2 * s, 2), :, k * depth:(k + 1) * depth] * weight[0]
            + qbuf[1, pl.ds(2 * s, 2), :, k * depth:(k + 1) * depth] * weight[1]
        ).reshape(2 * rows, depth)
        at = slice(k * depth, (k + 1) * depth)
        total = jnp.dot(pick, h_high[at], preferred_element_type=jnp.float32)
        total += jnp.dot(pick, h_low[at], preferred_element_type=jnp.float32)
        if k == 0:
            acc[...] = total
        elif k < PARTS - 1:
            acc[...] += total
        else:
            at = pl.ds(pl.multiple_of(s * 2 * rows, 2 * rows), 2 * rows)
            pbuf[core, at] = (acc[...] + total).astype(jnp.bfloat16)

    def pair_arrived(s):
        for k in range(PARTS):
            q_pair(s, k, 1 - core).wait_recv()

    def q_step(s, carry):
        pair_arrived(s - 1)
        for k in range(PARTS):
            q_ring(s - 1, k).wait_recv()
            q_ring(s, k).start()
            q_pair(s, k, core).start()
            fold(s - 1, k)
        return carry

    for k in range(PARTS):
        q_ring(0, k).wait_recv()
        q_ring(1, k).start()
        q_pair(1, k, core).start()
        load_h[k].wait()
        split_part(k)
        if k == 0:
            pair_arrived(0)
        fold(0, k)
    lax.fori_loop(2, RING - 1, q_step, 0)

    last = RING - 1
    for k in range(PARTS - 1):
        p_ring(0, k).start()
    pair_arrived(last - 1)
    for k in range(PARTS):
        q_ring(last - 1, k).wait_recv()
        q_pair(last, k, core).start()
        if k < PARTS - 1:
            p_pair(0, k, core).start()
        fold(last - 1, k)
    pair_arrived(last)
    for k in range(PARTS):
        fold(last, k)
    p_ring(0, PARTS - 1).start()
    p_pair(0, PARTS - 1, core).start()
    for copy in load_c:
        copy.wait()

    def score(s, which, low=0, high=PARTS):
        origin = pos - s + 2 * s * which
        block = block_of[device(origin, which)]
        start = low * part_rows
        result = lax.dot_general(
            pbuf[2 * s + which, start:high * part_rows], corpus[block], (((1,), (1,)), ((), ())),
            preferred_element_type=jnp.float32,
        )
        for i in range((high - low) * part_rows // rows):
            t, w = (start // rows + i) // 2, i % 2
            row = device(origin - t + 2 * t * w, w) * rows
            out[pl.ds(pl.multiple_of(row, rows), rows)] += result[i * rows:(i + 1) * rows]

    def p_arrived(s, low=0, high=PARTS):
        for k in range(low, high):
            p_pair(s, k, 1 - core).wait_recv()

    def p_step(s, carry):
        for k in range(PARTS):
            p_ring(s - 1, k).wait_recv()
            p_ring(s, k).start()
            p_pair(s, k, core).start()
            q_ring(s - 1, k).wait_send()
            q_pair(s - 1, k, core).wait_send()
            if k == 1:
                score(s - 1, core)
        p_arrived(s - 1)
        score(s - 1, 1 - core)
        return carry

    lax.fori_loop(1, last, p_step, 0)

    def p_sent(s, carry):
        for k in range(PARTS):
            p_ring(s, k).wait_send()
            p_pair(s, k, core).wait_send()
        return carry

    middle = PARTS // 2
    for k in range(PARTS):
        p_ring(last - 1, k).wait_recv()
        p_pair(last, k, core).start()
        if k == 0:
            score(last - 1, core)
            for i in range(PARTS):
                q_ring(last - 1, i).wait_send()
                q_pair(last - 1, i, core).wait_send()
                q_pair(last, i, core).wait_send()
        elif k == 1:
            p_arrived(last - 1)
            score(last - 1, 1 - core)
            lax.fori_loop(0, last - 2, p_sent, 0)
            score(last, core, 0, middle)
        elif k == 2:
            p_arrived(last, 0, k)
            score(last, 1 - core, 0, k)
            lax.fori_loop(last - 2, last, p_sent, 0)
            score(last, core, k, k + 1)
    score(last, core, PARTS - 1, PARTS)
    p_arrived(last, middle, PARTS)
    score(last, 1 - core, middle, PARTS)
    for k in range(PARTS):
        p_pair(last, k, core).wait_send()


def by_kernel(queries, hinv_slots, block_of, corpus_enc):
    rows, width = queries.shape
    _, mod_width, block_width = hinv_slots.shape
    held = corpus_enc.shape[0]
    slots = 2 * RING
    total = slots * rows
    sems = pltpu.SemaphoreType.DMA((RING, PARTS))
    anywhere = pl.BlockSpec(memory_space=pl.ANY)
    return pl.pallas_call(
        kernel,
        out_shape=pltpu.VMEM((total, held), jnp.float32),
        in_specs=[pl.BlockSpec(memory_space=pltpu.SMEM), anywhere, anywhere, anywhere],
        out_specs=pl.BlockSpec(memory_space=pltpu.VMEM),
        scratch_shapes=[
            pltpu.VMEM((rows, width), jnp.float32),
            pltpu.VMEM((mod_width, block_width), jnp.float32),
            pltpu.VMEM((mod_width, block_width), jnp.bfloat16),
            pltpu.VMEM((mod_width, block_width), jnp.bfloat16),
            pltpu.VMEM((slots, held, block_width), jnp.bfloat16),
            pltpu.VMEM((2, slots, rows, mod_width), jnp.bfloat16),
            pltpu.VMEM((slots, total, block_width), jnp.bfloat16),
            pltpu.VMEM((2 * rows, block_width), jnp.float32),
            pltpu.SemaphoreType.DMA((2 * PARTS,)),
            pltpu.SemaphoreType.DMA((slots,)),
        ] + [sems] * 8,
        compiler_params=pltpu.CompilerParams(
            collective_id=0, has_side_effects=True, vmem_limit_bytes=61 * 2**20
        ),
        cost_estimate=pl.CostEstimate(
            flops=2 * total * block_width * mod_width * 2 + 2 * total * held * width,
            bytes_accessed=20 * 2**20, transcendentals=0,
        ),
    )(block_of, queries, hinv_slots, corpus_enc)


def solution(mesh):
    devices = mesh.shape["corpus"]

    def on_device(queries, hinv_slots, block_of, corpus_enc):
        fits = (
            devices == 2 * RING
            and queries.shape[0] % 32 == 0
            and queries.shape[1] == 2 * hinv_slots.shape[1]
            and hinv_slots.shape[2] % 128 == 0
        )
        body = by_kernel if fits else by_collectives
        return body(queries, hinv_slots, block_of, corpus_enc)

    return jax.shard_map(
        on_device,
        mesh=mesh,
        in_specs=(
            P(("groups", "corpus"), None),
            P(("groups", "corpus"), None, None),
            P("groups"),
            P(("groups", "corpus"), None),
        ),
        out_specs=P(None, ("groups", "corpus")),
        check_vma=False,
    )
```
